256 devices in a mesh: leaf: 32 (over x, z), near: 8 (over y, core).
Axes of the slice: x: 4, y: 4, z: 8, core: 2. Of those that a mesh axis runs over, the one named last changes fastest.
Arguments:
- charges: bfloat16 [2048, 16, 128], P(('leaf', 'near')), may hold values from -6 to 6
- leaf_in: bfloat16 [2048, 64, 128], P(('leaf', 'near')), may hold values from -0.5 to 0.5
- leaf_out: bfloat16 [2048, 64, 128], P(('leaf', 'near')), may hold values from -0.75 to 0.75
- near_list: int32 [2048, 27], P(('leaf', 'near')), may hold values from 0 to 2047, as said below
- near_blocks: bfloat16 [2048, 27, 128, 128], P(('leaf', 'near')), may hold values from -0.109375 to 0.109375
- leaf_partners: int32 [2048, 8], P(('leaf', 'near')), may hold values from 0 to 2047, as said below
- leaf_couple: bfloat16 [2048, 64, 512], P(('leaf', 'near')), may hold values from -0.25 to 0.25
- leaf_up: bfloat16 [256, 64, 512], P(('leaf', 'near')), may hold values from -0.25 to 0.25
- leaf_down: bfloat16 [256, 64, 512], P(('leaf', 'near')), may hold values from -0.75 to 0.75
- box_partners: int32 [256, 8], P(('leaf', 'near')), may hold values from 0 to 255, as said below
- box_couple: bfloat16 [256, 64, 512], P(('leaf', 'near')), may hold values from -0.25 to 0.25
- box_transfer: bfloat16 [256, 64, 128], P(('leaf', 'near')), may hold values from -0.25 to 0.25
- top_partners: int32 [32, 8], P('leaf'), may hold values from 0 to 31
- top_couple: bfloat16 [32, 64, 512], P('leaf'), may hold values from -0.25 to 0.25
Outputs:
- potential: bfloat16 [2048, 16, 128], P(('leaf', 'near'))
The draws below stay inside these ranges and needn't reach their ends.
Inputs may be any that keep to these rules, and one draw needn't show every extreme that they name: `near_list`: leaves are numbered subtree by subtree, 8 to a device box and 8 device boxes to a subtree. Entry [l, s] names a leaf of the subtree of leaf l, or a leaf of the device box at the same place as l's box in the subtree just before or just after l's. Entries may repeat. `leaf_partners`: entry [l, c] names a leaf of the subtree of leaf l, or a leaf of the device box at the same place as l's box in the subtree just before or just after l's. Entries may repeat. `box_partners`: entry [b, c] names a device box of the subtree of box b. Entries may repeat.
All inputs are finite; a program needn't handle non-finite values.
Results may differ from the reference program's by a relative error of at most 0.015.
Values may be sent and summed in bfloat16 or wider, within the bound.
A program may use at most 64 MiB of HBM per device.

```python
import jax
import jax.numpy as jnp
from jax import lax

POINTS = 128
RANK = 64
RHS = 16
NEAR_SLOTS = 27
LEAF_PARTNERS = 8
BOX_PARTNERS = 8
TOP_PARTNERS = 8
LEAF_DEV = 8
BOX_SUB = 8
SUBTREES = 32
BOXES = 256
LEAVES = 2048


def window_leaves(key, slots):
    group_len = LEAF_DEV * BOX_SUB
    leaf_ids = jnp.arange(LEAVES, dtype=jnp.int32)[:, None]
    subtree = leaf_ids // group_len
    position = leaf_ids // LEAF_DEV % BOX_SUB
    picked = jax.random.randint(key, (LEAVES, slots), 0, group_len + 2 * LEAF_DEV, dtype=jnp.int32)
    own_leaf = subtree * group_len + picked % group_len
    lower_leaf = (subtree - 1) * group_len + position * LEAF_DEV + (picked - group_len)
    upper_leaf = (subtree + 1) * group_len + position * LEAF_DEV + (picked - group_len - LEAF_DEV)
    use_lower = (picked >= group_len) & (picked < group_len + LEAF_DEV) & (subtree > 0)
    use_upper = (picked >= group_len + LEAF_DEV) & (subtree < SUBTREES - 1)
    return jnp.where(use_lower, lower_leaf, jnp.where(use_upper, upper_leaf, own_leaf)).astype(jnp.int32)


def draw_near_list(key, part):
    return window_leaves(jax.random.fold_in(key, 11), NEAR_SLOTS)


def draw_leaf_partners(key, part):
    return window_leaves(jax.random.fold_in(key, 23), LEAF_PARTNERS)


def draw_box_partners(key, part):
    box_ids = jnp.arange(BOXES, dtype=jnp.int32)[:, None]
    picked = jax.random.randint(jax.random.fold_in(key, 37), (BOXES, BOX_PARTNERS), 0, BOX_SUB, dtype=jnp.int32)
    return (box_ids // BOX_SUB * BOX_SUB + picked).astype(jnp.int32)


def with_ends(entries, rng, low, largest):
    shape = entries.shape
    place = [jax.random.randint(jax.random.fold_in(rng, axis), (), 0, shape[axis]) for axis in range(len(shape))]
    entries = entries.at[tuple(place)].set(low)
    longest = shape.index(max(shape))
    place[longest] = (place[longest] + 1) % shape[longest]
    return entries.at[tuple(place)].set(largest)


def levels(rng, extent, shards, smallest, largest):
    def one(dim, shards_of):
        draws = jax.random.uniform(jax.random.fold_in(jax.random.fold_in(rng, 6), dim), (shards_of,), jnp.float32, smallest / len(shards), largest / len(shards))
        return jnp.repeat(jnp.exp(draws), extent[dim] // shards_of).reshape((-1,) + (1,) * (len(extent) - dim - 1))

    factor_of = one(*shards[0])
    for cut in shards[1:]:
        factor_of = factor_of * one(*cut)
    return factor_of


def bell_draw(rng, extent, deviation, reach, shards=(), kind=jnp.bfloat16):
    array = jax.random.normal(rng, extent, jnp.float32) * deviation
    if len(shards) > 0:
        array = levels(rng, extent, shards, -0.22, 0.18) * array
    return jnp.clip(array, min=-reach, max=reach).astype(kind)


def setup_inputs(seed: int = 0) -> dict:
    streams_of = jax.random.split(jax.random.key(seed), 15)
    return {
        "charges": bell_draw(streams_of[0], (LEAVES, RHS, POINTS), 1.0, 6.0, ((0, 256),)),
        "leaf_in": bell_draw(streams_of[1], (LEAVES, RANK, POINTS), POINTS ** -0.5, 0.5, ((0, 256),)),
        "leaf_out": bell_draw(streams_of[2], (LEAVES, RANK, POINTS), RANK ** -0.5, 0.75, ((0, 256),)),
        "near_list": draw_near_list(jax.random.fold_in(streams_of[14], 71), 0),
        "near_blocks": bell_draw(streams_of[4], (LEAVES, NEAR_SLOTS, POINTS, POINTS), (NEAR_SLOTS * POINTS) ** -0.5, 0.109375, ((0, 256),)),
        "leaf_partners": draw_leaf_partners(jax.random.fold_in(streams_of[14], 71), 0),
        "leaf_couple": bell_draw(streams_of[6], (LEAVES, RANK, LEAF_PARTNERS * RANK), (LEAF_PARTNERS * RANK) ** -0.5, 0.25, ((0, 256),)),
        "leaf_up": bell_draw(streams_of[7], (BOXES, RANK, LEAF_DEV * RANK), (LEAF_DEV * RANK) ** -0.5, 0.25, ((0, 256),)),
        "leaf_down": bell_draw(streams_of[8], (BOXES, RANK, LEAF_DEV * RANK), RANK ** -0.5, 0.75, ((0, 256),)),
        "box_partners": draw_box_partners(jax.random.fold_in(streams_of[14], 71), 0),
        "box_couple": bell_draw(streams_of[10], (BOXES, RANK, BOX_PARTNERS * RANK), (BOX_PARTNERS * RANK) ** -0.5, 0.25, ((0, 256),)),
        "box_transfer": bell_draw(streams_of[11], (BOXES, RANK, 2 * RANK), (RANK * BOX_SUB) ** -0.5, 0.25, ((0, 256),)),
        "top_partners": with_ends(jax.random.randint(streams_of[12], (SUBTREES, TOP_PARTNERS), 0, SUBTREES), jax.random.fold_in(streams_of[12], 1), 0, SUBTREES - 1).astype(jnp.int32),
        "top_couple": bell_draw(streams_of[13], (SUBTREES, RANK, TOP_PARTNERS * RANK), (TOP_PARTNERS * RANK) ** -0.5, 0.25, ((0, 32),)),
    }


def side_by_side(table, partners):
    picked = table[partners].astype(jnp.float32)
    count = partners.shape[0]
    return picked.transpose(0, 2, 1, 3).reshape(count, RHS, partners.shape[1] * RANK)


def reference(charges, leaf_in, leaf_out, near_list, near_blocks, leaf_partners, leaf_couple, leaf_up, leaf_down, box_partners, box_couple, box_transfer, top_partners, top_couple):
    moments = jnp.einsum('lrp,lkp->lrk', charges.astype(jnp.float32), leaf_in.astype(jnp.float32)).astype(jnp.bfloat16)
    stacked = moments.astype(jnp.float32).reshape(BOXES, LEAF_DEV, RHS, RANK).transpose(0, 2, 1, 3).reshape(BOXES, RHS, LEAF_DEV * RANK)
    box_moments = jnp.einsum('bri,boi->bro', stacked, leaf_up.astype(jnp.float32)).astype(jnp.bfloat16)
    transfer = box_transfer.astype(jnp.float32)
    shares = jnp.einsum('brk,bko->bro', box_moments.astype(jnp.float32), transfer[:, :, :RANK]).astype(jnp.bfloat16)
    subtree_moments = shares.astype(jnp.float32).reshape(SUBTREES, BOX_SUB, RHS, RANK).sum(axis=1).astype(jnp.bfloat16)
    top_in = side_by_side(subtree_moments, top_partners)
    top_local = jnp.einsum('sri,soi->sro', top_in, top_couple.astype(jnp.float32)).astype(jnp.bfloat16)
    box_in = side_by_side(box_moments, box_partners)
    parent = jnp.repeat(top_local.astype(jnp.float32), BOX_SUB, axis=0)
    box_local = (jnp.einsum('bri,boi->bro', box_in, box_couple.astype(jnp.float32)) + jnp.einsum('brk,bko->bro', parent, transfer[:, :, RANK:])).astype(jnp.bfloat16)
    leaf_in_moments = side_by_side(moments, leaf_partners)
    from_box = jnp.einsum('brk,bki->bri', box_local.astype(jnp.float32), leaf_down.astype(jnp.float32))
    from_box = from_box.reshape(BOXES, RHS, LEAF_DEV, RANK).transpose(0, 2, 1, 3).reshape(LEAVES, RHS, RANK)
    leaf_local = (jnp.einsum('lri,loi->lro', leaf_in_moments, leaf_couple.astype(jnp.float32)) + from_box).astype(jnp.bfloat16)
    far_field = jnp.einsum('lrk,lkq->lrq', leaf_local.astype(jnp.float32), leaf_out.astype(jnp.float32))

    def near_box(box_index):
        start = (box_index * LEAF_DEV).astype(jnp.int32)
        slot_rows = lax.dynamic_slice_in_dim(near_list, start, LEAF_DEV, 0)
        blocks = lax.dynamic_slice_in_dim(near_blocks, start, LEAF_DEV, 0).astype(jnp.float32)
        gathered = charges[slot_rows].astype(jnp.float32)
        return jnp.einsum('lsrp,lspq->lrq', gathered, blocks)

    near_field = lax.map(near_box, jnp.arange(BOXES, dtype=jnp.int32)).reshape(LEAVES, RHS, POINTS)
    return (near_field + far_field).astype(jnp.bfloat16)
```

```python
import functools

import jax
import jax.numpy as jnp
from jax import lax
from jax.experimental import pallas as pl
from jax.experimental.pallas import tpu as pltpu
from jax.sharding import PartitionSpec as P

MESH = pl.DeviceIdType.MESH
F32 = jnp.float32
BF16 = jnp.bfloat16


def torus_offsets(nx, nz):
    def hops(dx, dz):
        return min(dx, nx - dx) + min(dz, nz - dz)

    every = [(dx, dz) for dx in range(nx) for dz in range(nz) if dx or dz]
    return sorted(every, key=lambda o: -hops(*o))


def dot_nt(a, b):
    return lax.dot_general(a, b, (((1,), (1,)), ((), ())), preferred_element_type=F32)


def dot_nn(a, b):
    return jnp.dot(a, b, preferred_element_type=F32)


def kernel(
    nx,
    nz,
    nn,
    charges,
    leaf_in,
    leaf_out,
    near_list,
    near_blocks,
    leaf_partners,
    leaf_couple,
    leaf_up,
    leaf_down,
    box_partners,
    box_couple,
    box_transfer,
    top_partners,
    top_couple,
    out,
    cwin,
    mpair,
    mwin,
    bs,
    bmd,
    topb,
    li,
    lo,
    nb,
    lc,
    lu,
    ld,
    bc,
    bt,
    tc,
    nl,
    lp,
    bp,
    tp,
    near,
    coup,
    lsem,
    nsem,
    near_ssem,
    near_rsem,
    leaf_ssem,
    leaf_rsem,
    far_ssem,
    far_rsem,
):
    ns = nx * nz
    s = lax.axis_index("leaf")
    n = lax.axis_index("near")
    x = s // nz
    z = s % nz
    far = torus_offsets(nx, nz)
    group = 8 * nn
    ring = 4 * group
    place = [(s + i + 3) % 4 * group + n * 8 for i in range(3)]
    own, own_pair = place[1], place[1] // 2

    local = []

    def load(src, dst, sem):
        cp = pltpu.make_async_copy(src, dst, sem)
        cp.start()
        return cp

    c_ch = load(charges, cwin.at[pl.ds(own, 8)], lsem.at[0])
    c_li = load(leaf_in, li, lsem.at[1])
    c_lu0 = load(leaf_up.at[0], lu.at[pl.ds(0, 64)], lsem.at[2])
    c_lu1 = load(leaf_up.at[0], lu.at[pl.ds(64, 64)], lsem.at[3])
    c_bt = load(box_transfer.at[0], bt, lsem.at[4])

    barrier = pltpu.get_barrier_semaphore()
    for dx, dz in far:
        pl.semaphore_signal(
            barrier, 1, device_id=(((x + dx) % nx) * nz + (z + dz) % nz, n), device_id_type=MESH
        )
    for d in range(1, nn):
        pl.semaphore_signal(barrier, 1, device_id=(s, (n + d) % nn), device_id_type=MESH)

    c_nl = load(near_list, nl, lsem.at[5])
    c_lp = load(leaf_partners, lp, lsem.at[6])
    c_bp = load(box_partners, bp, lsem.at[7])
    c_tp = load(top_partners, tp, lsem.at[8])
    c_bc = load(box_couple.at[0], bc, lsem.at[9])
    c_tc = load(top_couple.at[0], tc, lsem.at[10])
    c_ld = load(leaf_down.at[0], ld, lsem.at[11])
    c_lc = load(leaf_couple, lc, lsem.at[12])
    c_lo = load(leaf_out, lo, lsem.at[13])
    c_nb = [load(near_blocks.at[i], nb.at[i], nsem.at[i]) for i in range(8)]

    low = lax.broadcasted_iota(jnp.int32, (16, 128), 1) < 64

    def pick(a, b):
        return jnp.where(low, a, b)

    c_ch.wait()
    c_li.wait()
    tiles = []
    for t in range(4):
        two = cwin[pl.ds(own + 2 * t, 2)].reshape(32, 128)
        m = dot_nt(two, li[2 * t : 2 * t + 2].reshape(128, 128))
        tile = pick(m[:16], m[16:]).astype(BF16)
        mpair[own_pair + t] = tile
        tiles.append(tile)
    c_lu0.wait()
    c_lu1.wait()
    c_bt.wait()
    box2 = dot_nt(jnp.concatenate(tiles, axis=1), lu[...])
    flipped = pltpu.roll(bt[...].astype(F32), 64, 1).astype(BF16)
    share = dot_nn(box2.astype(BF16)[:, :64], flipped)
    bs[n] = pick(box2, share).astype(BF16)

    pl.semaphore_wait(barrier, len(far) + nn - 1)

    sends = []

    def send(src, dst, ssem, rsem, to):
        cp = pltpu.make_async_remote_copy(
            src_ref=src, dst_ref=dst, send_sem=ssem, recv_sem=rsem, device_id=to, device_id_type=MESH
        )
        cp.start()
        sends.append(cp)
        return cp

    order = sorted(range(1, nn), key=lambda d: -min(d, nn - d))
    r_bs = [
        send(bs.at[n], bs.at[n], near_ssem.at[0, d], near_rsem.at[0, d], (s, (n + d) % nn)) for d in order
    ]
    mine = cwin.at[pl.ds(own, 8)]
    mine_pairs = mpair.at[pl.ds(own_pair, 4)]
    r_ch = [
        send(mine, mine, near_ssem.at[1, d], near_rsem.at[1, d], (s, (n + d) % nn)) for d in order
    ]
    upper = ((s + 1) % ns, n)
    lower = ((s + ns - 1) % ns, n)
    r_ch.append(send(mine, mine, leaf_ssem.at[0], leaf_rsem.at[0], upper))
    r_ch.append(send(mine, mine, leaf_ssem.at[1], leaf_rsem.at[1], lower))
    r_mo = [
        send(mine_pairs, mine_pairs, near_ssem.at[2, d], near_rsem.at[2, d], (s, (n + d) % nn))
        for d in order
    ]
    r_mo.append(send(mine_pairs, mine_pairs, leaf_ssem.at[2], leaf_rsem.at[2], upper))
    r_mo.append(send(mine_pairs, mine_pairs, leaf_ssem.at[3], leaf_rsem.at[3], lower))

    for cp in r_bs:
        cp.wait_recv()
    total = bs[0].astype(F32)
    for i in range(1, nn):
        total = total + bs[i].astype(F32)
    topb[s] = pick(pltpu.roll(total, 64, 1), total).astype(BF16)
    r_far = [
        send(
            topb.at[s],
            topb.at[s],
            far_ssem.at[i],
            far_rsem.at[i],
            (((x + dx) % nx) * nz + (z + dz) % nz, n),
        )
        for i, (dx, dz) in enumerate(far)
    ]

    for i in range(nn):
        b = bs[i].astype(F32)
        bmd[i] = pick(b, pltpu.roll(b, 64, 1)).astype(BF16)
    c_bp.wait()
    c_bc.wait()

    def beside(table, ids):
        return jnp.concatenate([pick(table(ids[2 * t]), table(ids[2 * t + 1])) for t in range(4)], axis=1)

    box_in = beside(lambda i: bmd[i], [bp[0, c] & (nn - 1) for c in range(8)])
    box_part = dot_nt(box_in, bc[...])

    for cp in r_mo:
        cp.wait_recv()

    def spread(q):
        p = mpair[q].astype(F32)
        r = pltpu.roll(p, 64, 1)
        mwin[q, 0] = pick(p, r).astype(BF16)
        mwin[q, 1] = pick(r, p).astype(BF16)

    def spread_own(i, c):
        for j in range(4):
            spread(own_pair - n * 4 + i * 4 + j)
        return c

    lax.fori_loop(0, nn, spread_own, 0)
    for j in range(4):
        spread(place[0] // 2 + j)
        spread(place[2] // 2 + j)
    c_lp.wait()
    c_lc.wait()

    def moment_of(leaf):
        return mwin[(leaf & (ring - 1)) >> 1, leaf & 1]

    for t in range(4):
        rows = [beside(moment_of, [lp[2 * t + h, c] for c in range(8)]) for h in range(2)]
        m = dot_nt(jnp.concatenate(rows, axis=0), lc[2 * t : 2 * t + 2].reshape(128, 512))
        coup[t] = pick(m[:16], m[16:])

    for cp in r_ch:
        cp.wait_recv()
    c_nl.wait()

    def near_leaf(i, c):
        pltpu.make_async_copy(near_blocks.at[i], nb.at[i], nsem.at[i]).wait()
        rows = jnp.concatenate([cwin[nl[i, k] & (ring - 1)] for k in range(27)], axis=1)
        near[i] = dot_nn(rows, nb[i].reshape(27 * 128, 128))
        return c

    lax.fori_loop(0, 8, near_leaf, 0)

    c_tp.wait()
    c_tc.wait()
    c_ld.wait()
    c_lo.wait()
    for cp in r_far:
        cp.wait_recv()
    top_in = beside(lambda i: topb[i], [tp[0, c] & (ns - 1) for c in range(8)])
    top_local = dot_nt(top_in, tc[...]).astype(BF16)
    from_top = dot_nn(top_local, flipped)[:, :64]
    box_local = (box_part + from_top).astype(BF16)
    from_box = dot_nn(box_local, ld[...])
    zero = jnp.zeros((16, 128), F32)
    for t in range(4):
        both = coup[t] + from_box[:, t * 128 : (t + 1) * 128]
        rows = jnp.concatenate([pick(both, zero), pick(zero, both)], axis=0).astype(BF16)
        o = dot_nn(rows, lo[2 * t : 2 * t + 2].reshape(128, 128))
        out[2 * t] = (near[2 * t] + o[:16]).astype(BF16)
        out[2 * t + 1] = (near[2 * t + 1] + o[16:]).astype(BF16)

    for cp in sends:
        cp.wait_send()


def per_device(nx, nz, nn, *args):
    ns = nx * nz
    group = 8 * nn
    n_far = ns - 1
    dma = pltpu.SemaphoreType.DMA
    scratch = [
        pltpu.VMEM((4 * group, 16, 128), BF16),
        pltpu.VMEM((4 * group // 2, 16, 128), BF16),
        pltpu.VMEM((4 * group // 2, 2, 16, 128), BF16),
        pltpu.VMEM((nn, 16, 128), BF16),
        pltpu.VMEM((nn, 16, 128), BF16),
        pltpu.VMEM((ns, 16, 128), BF16),
        pltpu.VMEM((8, 64, 128), BF16),
        pltpu.VMEM((8, 64, 128), BF16),
        pltpu.VMEM((8, 27, 128, 128), BF16),
        pltpu.VMEM((8, 64, 512), BF16),
        pltpu.VMEM((128, 512), BF16),
        pltpu.VMEM((64, 512), BF16),
        pltpu.VMEM((64, 512), BF16),
        pltpu.VMEM((64, 128), BF16),
        pltpu.VMEM((64, 512), BF16),
        pltpu.SMEM((8, 27), jnp.int32),
        pltpu.SMEM((8, 8), jnp.int32),
        pltpu.SMEM((1, 8), jnp.int32),
        pltpu.SMEM((1, 8), jnp.int32),
        pltpu.VMEM((8, 16, 128), F32),
        pltpu.VMEM((4, 16, 128), F32),
        dma((14,)),
        dma((8,)),
        dma((3, nn)),
        dma((3, nn)),
        dma((4,)),
        dma((4,)),
        dma((n_far,)),
        dma((n_far,)),
    ]
    return pl.pallas_call(
        functools.partial(kernel, nx, nz, nn),
        out_shape=jax.ShapeDtypeStruct((8, 16, 128), BF16),
        in_specs=[pl.BlockSpec(memory_space=pltpu.HBM)] * len(args),
        out_specs=pl.BlockSpec(memory_space=pltpu.VMEM),
        scratch_shapes=scratch,
        compiler_params=pltpu.CompilerParams(
            collective_id=0, has_side_effects=True, vmem_limit_bytes=32 * 2**20
        ),
        name="h2_product",
    )(*args)


def solution(mesh):
    ns, nn = mesh.shape["leaf"], mesh.shape["near"]
    nz = 8 if ns % 8 == 0 else ns
    both = ("leaf", "near")
    return jax.shard_map(
        functools.partial(per_device, ns // nz, nz, nn),
        mesh=mesh,
        in_specs=(
            P(both, None, None),
            P(both, None, None),
            P(both, None, None),
            P(both, None),
            P(both, None, None, None),
            P(both, None),
            P(both, None, None),
            P(both, None, None),
            P(both, None, None),
            P(both, None),
            P(both, None, None),
            P(both, None, None),
            P("leaf", None),
            P("leaf", None, None),
        ),
        out_specs=P(both, None, None),
        check_vma=False,
    )
```
